32 devices in a mesh: dp: 4 (over z), seq: 8 (over y, x, core).
Axes of the slice: x: 2, y: 2, z: 4, core: 2. Of those that a mesh axis runs over, the one named last changes fastest.
Arguments:
- inputs: bfloat16 [4, 2048, 5120], P('dp', 'seq'), may hold values from -6 to 6
- gate_proj: bfloat16 [4, 2048, 5120], P('dp', 'seq'), may hold values from -6 to 6
- write_proj: bfloat16 [4, 2048, 128], P('dp', 'seq'), may hold values from -6 to 6
- read_proj: bfloat16 [4, 2048, 128], P('dp', 'seq'), may hold values from -6 to 6
- step_size: float32 [4, 80, 2048], P('dp', None, 'seq'), may hold values from 0 to 0.4, as said below
- log_forget: float32 [4, 80, 2048], P('dp', None, 'seq'), may hold values from -0.8 to 0, as said below
- conv_weight: float32 [4, 5376], replicated, may hold values from -3 to 3
- conv_bias: float32 [5376], replicated, may hold values from -3 to 3
- skip_gain: float32 [80], replicated, may hold values from 0.5 to 1.5
- norm_gain: float32 [5120], replicated, may hold values from 0.1 to 1.9
- code_weight: bfloat16 [5120, 256], P('dp'), may hold values from -0.5 to 0.5
- prior_draw: float32 [256, 256], P(('dp', 'seq')), may hold values from -6 to 6
Outputs:
- mixed: bfloat16 [4, 2048, 5120], P('dp', 'seq')
- codes: float32 [256, 256], P(('dp', 'seq'))
- kernel: float32 [256, 512], P(('dp', 'seq'))
The draws below stay inside these ranges and needn't reach their ends.
Inputs may be any that keep to these rules, and one draw needn't show every extreme that they name: `step_size`: positive step sizes, per document, head and position. `log_forget`: never positive.
All inputs are finite; a program needn't handle non-finite values.
Results may differ from the reference program's by a relative error of at most 0.008.
Values may be sent and summed in bfloat16 or wider, within the bound.
A program may use at most 256 MiB of HBM per device.

```python
import math
import jax
import jax.numpy as jnp
from jax import lax

HEADS = 80
HEAD_DIM = 64
STATE = 128
CONV = 4
SPAN = 128
ZD = 256
SEG = 32
L_DEV = 256
CORPUS_SIZE = 4
TOKEN_SPAN = 2048
DI = 5120
CODES = 256


def decay_plan(key):
    base = jax.random.fold_in(key, 7)
    slow_share = 0.5
    medium_share = 0.8
    pick = jax.random.uniform(jax.random.fold_in(base, 1), (HEADS,), jnp.float32)
    slow_rate = 0.4 / TOKEN_SPAN * jnp.exp(jax.random.uniform(jax.random.fold_in(base, 2), (HEADS,), jnp.float32, -0.693, 0.693))
    fast_rate = jnp.exp(jax.random.uniform(jax.random.fold_in(base, 3), (HEADS,), jnp.float32, jnp.log(1.0 / 50.0), jnp.log(1.0 / 20.0)))
    medium_rate = jnp.exp(jax.random.uniform(jax.random.fold_in(base, 4), (HEADS,), jnp.float32, jnp.log(1.5 / L_DEV), jnp.log(3.5 / L_DEV)))
    medium_rate = jnp.minimum(medium_rate, 0.05)
    return jnp.where(pick < slow_share, slow_rate, jnp.where(pick < medium_share, medium_rate, fast_rate))


def draw_log_forget(key, part):
    forgetting_factors = decay_plan(key)
    device_entries = jax.random.fold_in(key, 31)
    rough_approximation = jnp.exp(jax.random.uniform(jax.random.fold_in(device_entries, 1), (CORPUS_SIZE, HEADS, TOKEN_SPAN), jnp.float32, -0.693, 0.693))
    chosen_flare = jax.random.uniform(jax.random.fold_in(device_entries, 2), (CORPUS_SIZE, 1, TOKEN_SPAN), jnp.float32)
    recursion_levels = jax.random.uniform(jax.random.fold_in(device_entries, 3), (CORPUS_SIZE, 1, TOKEN_SPAN), jnp.float32, 0.22, 0.7)
    flare_clusters = jnp.where(chosen_flare < 3.0 / TOKEN_SPAN, recursion_levels, 0.0)
    return -(forgetting_factors[None, :, None] * rough_approximation) - flare_clusters


def draw_step_size(key, part):
    forgetting_factors = decay_plan(key)
    device_entries = jax.random.fold_in(key, 41)
    base = jnp.exp(jax.random.uniform(device_entries, (CORPUS_SIZE, HEADS, TOKEN_SPAN), jnp.float32, jnp.log(0.05), jnp.log(0.2)))
    return base * jnp.minimum(40.0 * forgetting_factors, 2.0)[None, :, None]


def shared_channels(key, channel_seed, width):
    factor_count = 6
    amplitude = 1.0
    noise_part = jax.random.normal(jax.random.fold_in(key, channel_seed + 1), (CORPUS_SIZE, TOKEN_SPAN, width), jnp.float32)
    factors = jax.random.normal(jax.random.fold_in(key, 101), (CORPUS_SIZE, TOKEN_SPAN, factor_count), jnp.float32)
    loadings = jax.random.normal(jax.random.fold_in(key, channel_seed), (CORPUS_SIZE, factor_count, width), jnp.float32)
    weight_each = amplitude / math.sqrt(factor_count)
    result = noise_part
    for factor_index in range(factor_count):
        result = result + weight_each * factors[:, :, factor_index:factor_index + 1] * loadings[:, factor_index:factor_index + 1, :]
    return jnp.clip(result, -6.0, 6.0).astype(jnp.bfloat16)


def draw_inputs(key, part):
    return shared_channels(key, 211, DI)


def draw_write_proj(key, part):
    return shared_channels(key, 307, STATE)


def shard_levels(own_key, shape, split, least, top_value):
    def one(axis_at, shards_of):
        heights = jax.random.uniform(jax.random.fold_in(jax.random.fold_in(own_key, 6), axis_at), (shards_of,), jnp.float32, least / len(split), top_value / len(split))
        return jnp.repeat(jnp.exp(heights), shape[axis_at] // shards_of).reshape((-1,) + (1,) * (len(shape) - axis_at - 1))

    factor_of = one(*split[0])
    for cut in split[1:]:
        factor_of = factor_of * one(*cut)
    return factor_of


def noise(stream_key, extent, scale, bound, cuts=(), kind=jnp.bfloat16):
    drawn = scale * jax.random.normal(stream_key, extent, jnp.float32)
    if cuts:
        drawn = drawn * shard_levels(stream_key, extent, cuts, -0.22, 0.18)
    return jnp.clip(drawn, -bound, bound).astype(kind)


def setup_inputs(seed: int = 0) -> dict:
    arg_keys = jax.random.split(jax.random.key(seed), 13)
    inputs = draw_inputs(jax.random.fold_in(arg_keys[12], 71), 0)
    gate_proj = noise(arg_keys[1], (CORPUS_SIZE, TOKEN_SPAN, DI), 1.0, 6.0, ((0, 4), (1, 8)))
    write_proj = draw_write_proj(jax.random.fold_in(arg_keys[12], 71), 0)
    read_proj = noise(arg_keys[3], (CORPUS_SIZE, TOKEN_SPAN, STATE), 1.0, 6.0, ((0, 4), (1, 8)))
    step_size = draw_step_size(jax.random.fold_in(arg_keys[12], 71), 0)
    log_forget = draw_log_forget(jax.random.fold_in(arg_keys[12], 71), 0)
    conv_weight = noise(arg_keys[6], (CONV, DI + 2 * STATE), CONV ** -0.5, 3.0, (), jnp.float32)
    conv_bias = noise(arg_keys[7], (DI + 2 * STATE,), 0.5, 3.0, (), jnp.float32)
    skip_gain = jnp.clip(jax.random.uniform(arg_keys[8], (HEADS,), jnp.float32, 0.5, 1.5), 0.5, 1.5)
    norm_gain = jnp.clip(1.0 + 0.18 * jax.random.normal(arg_keys[9], (DI,), jnp.float32), 0.1, 1.9)
    code_weight = noise(arg_keys[10], (DI, ZD), (DI // SEG) ** -0.5, 0.5, ((0, 4),))
    prior_draw = noise(arg_keys[11], (CODES, ZD), 1.0, 6.0, ((0, 32),), jnp.float32)
    return dict(inputs=inputs, gate_proj=gate_proj, write_proj=write_proj, read_proj=read_proj, step_size=step_size, log_forget=log_forget, conv_weight=conv_weight, conv_bias=conv_bias, skip_gain=skip_gain, norm_gain=norm_gain, code_weight=code_weight, prior_draw=prior_draw)


def block_terms(values, write_f, read_f, steps, logs):
    cum_log = jnp.cumsum(logs, axis=1)
    length = logs.shape[1]
    causal = jnp.arange(length)[:, None] >= jnp.arange(length)[None, :]
    scores = jnp.dot(read_f, write_f.T, precision=lax.Precision.HIGHEST)
    gap = jnp.where(causal[None], cum_log[:, :, None] - cum_log[:, None, :], 0.0)
    mixing = jnp.where(causal[None], scores[None] * jnp.exp(gap) * steps[:, None, :], 0.0)
    mixing = lax.optimization_barrier(mixing.astype(jnp.bfloat16)).astype(jnp.float32)
    inner_out = jnp.einsum('hts,shp->thp', mixing, values, precision=lax.Precision.HIGHEST)
    tail_decay = jnp.exp(cum_log[:, -1:] - cum_log) * steps
    weighted = tail_decay[:, :, None] * write_f[None]
    weighted = lax.optimization_barrier(weighted.astype(jnp.bfloat16)).astype(jnp.float32)
    states = jnp.einsum('hsn,shp->hpn', weighted, values, precision=lax.Precision.HIGHEST)
    return (inner_out, states, cum_log)

def document(pieces, conv_weight, conv_bias, skip_gain, norm_gain):
    inputs_doc, gate_doc, write_doc, read_doc, steps_doc, logs_doc = pieces
    blocks = TOKEN_SPAN // SPAN
    joined = jnp.concatenate([inputs_doc, write_doc, read_doc], axis=1).astype(jnp.float32)
    padded = jnp.pad(joined, ((CONV - 1, 0), (0, 0)))
    summed = conv_bias[None, :] + jnp.zeros_like(joined)
    for offset in range(CONV):
        summed = summed + conv_weight[offset][None, :] * padded[offset:offset + TOKEN_SPAN]
    active = jax.nn.silu(summed).astype(jnp.bfloat16).astype(jnp.float32)
    values = active[:, :DI].reshape(blocks, SPAN, HEADS, HEAD_DIM)
    write_f = active[:, DI:DI + STATE].reshape(blocks, SPAN, STATE)
    read_f = active[:, DI + STATE:].reshape(blocks, SPAN, STATE)
    steps = steps_doc.reshape(HEADS, blocks, SPAN).transpose(1, 0, 2)
    logs = logs_doc.reshape(HEADS, blocks, SPAN).transpose(1, 0, 2)

    def advance(carry, block_pieces):
        values_b, write_b, read_b, steps_b, logs_b = block_pieces
        inner_out, states, cum_log = block_terms(values_b, write_b, read_b, steps_b, logs_b)
        outer_out = jnp.exp(cum_log).T[:, :, None] * jnp.einsum('tn,hpn->thp', read_b, carry, precision=lax.Precision.HIGHEST)
        carry_next = jnp.exp(cum_log[:, -1])[:, None, None] * carry + states
        return (carry_next, inner_out + outer_out)
    start = jnp.zeros((HEADS, HEAD_DIM, STATE), jnp.float32)
    final_state, ssd_out = lax.scan(advance, start, (values, write_f, read_f, steps, logs))
    ssd_out = ssd_out.reshape(TOKEN_SPAN, HEADS, HEAD_DIM)
    total = ssd_out + skip_gain[None, :, None] * values.reshape(TOKEN_SPAN, HEADS, HEAD_DIM)
    gated = total.reshape(TOKEN_SPAN, DI) * jax.nn.silu(gate_doc.astype(jnp.float32))
    scale = lax.rsqrt(lax.optimization_barrier(jnp.mean(gated * gated, axis=1, keepdims=True)) + 1e-05)
    mixed_doc = (gated * scale * norm_gain[None, :]).astype(jnp.bfloat16)
    pooled = lax.optimization_barrier(jnp.mean(mixed_doc.astype(jnp.float32).reshape(TOKEN_SPAN // SEG, SEG, DI), axis=1)).astype(jnp.bfloat16)
    return (mixed_doc, pooled)

def reference(inputs, gate_proj, write_proj, read_proj, step_size, log_forget, conv_weight, conv_bias, skip_gain, norm_gain, code_weight, prior_draw):

    def one_doc(pieces):
        return document(pieces, conv_weight, conv_bias, skip_gain, norm_gain)
    mixed, pooled = lax.map(one_doc, (inputs, gate_proj, write_proj, read_proj, step_size, log_forget))
    codes = jnp.dot(pooled.reshape(CODES, DI), code_weight, preferred_element_type=jnp.float32)
    columns = jnp.concatenate([codes, prior_draw], axis=0)
    cross = jnp.dot(codes, columns.T, precision=lax.Precision.HIGHEST)
    row_sq = lax.optimization_barrier(jnp.sum(codes * codes, axis=1))
    col_sq = lax.optimization_barrier(jnp.sum(columns * columns, axis=1))
    dist_sq = row_sq[:, None] + col_sq[None, :] - 2.0 * cross
    kernel = 2.0 * ZD / (2.0 * ZD + dist_sq)
    return (mixed, codes, kernel)
```

```python
import functools

import jax
import jax.numpy as jnp
from jax import lax
from jax.experimental import pallas as pl
from jax.experimental.pallas import tpu as pltpu
from jax.sharding import PartitionSpec as P

SPAN = 128
SEG = 32
LANES = 128
CHUNK = 512
F32 = jnp.float32
BF16 = jnp.bfloat16
HIGH = lax.Precision.HIGHEST
MESH = pl.DeviceIdType.MESH
NT = (((1,), (1,)), ((), ()))


def silu(v):
    half = 0.5 * v
    return half + half * jnp.tanh(half)


def dot(a, b):
    return jnp.dot(a, b, preferred_element_type=F32)


def spread(rows, shift, unit):
    turned = pltpu.roll(rows, shift, 1)
    upper = turned.astype(BF16)
    lower = (turned - upper.astype(F32)).astype(BF16)
    return dot(jnp.concatenate([upper, lower], axis=1), unit)


def mixer_kernel(
    n_seq,
    head_dim,
    x_ref,
    gate_ref,
    write_ref,
    read_ref,
    steps_ref,
    logs_ref,
    taps_ref,
    bias_ref,
    skip_ref,
    gain_ref,
    mixed_ref,
    pooled_ref,
    rim_x,
    rim_w,
    rim_r,
    pad,
    values,
    total,
    inner_state,
    own_state,
    came,
    leaving,
    cum,
    cum_t,
    tail_t,
    grow_t,
    decays,
    unit,
    scores,
    write_t,
    reads,
    squares,
    scale,
    rim_send,
    rim_recv,
    send_sem,
    recv_sem,
):
    length, width = x_ref.shape
    heads = steps_ref.shape[0]
    taps = taps_ref.shape[0]
    chunks = width // CHUNK
    per_chunk = CHUNK // head_dim
    blocks = length // SPAN
    place = lax.axis_index("seq")
    has_left = place > 0
    has_right = place < n_seq - 1
    left = {"seq": jnp.maximum(place - 1, 0)}
    right = {"seq": jnp.minimum(place + 1, n_seq - 1)}

    barrier = pltpu.get_barrier_semaphore()

    @pl.when(has_left)
    def _():
        pl.semaphore_signal(barrier, inc=1, device_id=left, device_id_type=MESH)

    @pl.when(has_right)
    def _():
        pl.semaphore_signal(barrier, inc=1, device_id=right, device_id_type=MESH)

    neighbours = jnp.minimum(place, 1) + jnp.minimum(n_seq - 1 - place, 1)
    pl.semaphore_wait(barrier, neighbours)

    def rims():
        return [
            pltpu.make_async_remote_copy(
                src_ref=source.at[pl.ds(length - 16, 16)],
                dst_ref=target,
                send_sem=rim_send.at[k],
                recv_sem=rim_recv.at[k],
                device_id=right,
                device_id_type=MESH,
            )
            for k, (source, target) in enumerate(
                ((x_ref, rim_x), (write_ref, rim_w), (read_ref, rim_r))
            )
        ]

    def passing(j):
        return pltpu.make_async_remote_copy(
            src_ref=leaving.at[j],
            dst_ref=came.at[j],
            send_sem=send_sem.at[j],
            recv_sem=recv_sem.at[j],
            device_id=right,
            device_id_type=MESH,
        )

    @pl.when(has_right)
    def _():
        for copy in rims():
            copy.start()

    row = lax.broadcasted_iota(jnp.int32, (SPAN, SPAN), 0)
    col = lax.broadcasted_iota(jnp.int32, (SPAN, SPAN), 1)
    below = (row >= col).astype(F32)
    same = (row == col).astype(F32)
    cum[...] = jnp.zeros_like(cum)
    decays[...] = jnp.zeros_like(decays)
    pad_heads = jnp.zeros((LANES - heads, SPAN), F32)
    for b in range(blocks):
        span = pl.ds(b * SPAN, SPAN)
        logs = jnp.concatenate([logs_ref[:, span], pad_heads], axis=0)
        steps = jnp.concatenate([steps_ref[:, span], pad_heads], axis=0)
        cum[:, span] = lax.dot_general(logs, below, NT, precision=HIGH, preferred_element_type=F32)
        by_time = lax.dot_general(below, logs, NT, precision=HIGH, preferred_element_type=F32)
        steps_t = lax.dot_general(same, steps, NT, precision=HIGH, preferred_element_type=F32)
        cum_t[span, :] = by_time
        grow_t[span, :] = jnp.exp(by_time)
        tail_t[span, :] = jnp.exp(jnp.minimum(by_time[SPAN - 1 :, :] - by_time, 0.0)) * steps_t
        decays[b : b + 1, :] = jnp.exp(by_time[SPAN - 1 :, :])
    decays[blocks : blocks + 1, 0:heads] = skip_ref[...]
    k = lax.broadcasted_iota(jnp.int32, (2 * LANES, CHUNK), 0)
    c = lax.broadcasted_iota(jnp.int32, (2 * LANES, CHUNK), 1)
    unit[...] = jnp.where(k % LANES == c // head_dim, 1.0, 0.0).astype(BF16)
    squares[...] = jnp.zeros_like(squares)

    @pl.when(has_left)
    def _():
        for copy in rims():
            copy.wait_recv()

    @pl.when(jnp.logical_not(has_left))
    def _():
        rim_x[...] = jnp.zeros_like(rim_x)
        rim_w[...] = jnp.zeros_like(rim_w)
        rim_r[...] = jnp.zeros_like(rim_r)
        came[...] = jnp.zeros_like(came)

    def convolved(rim, body, columns, size):
        pad[0:8, 0:size] = rim.astype(F32)[8:16]
        pad[8 : 8 + length, 0:size] = body.astype(F32)
        result = bias_ref[:, columns] + taps_ref[taps - 1 : taps, columns] * body.astype(F32)
        for tap in range(taps - 1):
            shifted = pad[pl.ds(8 - (taps - 1) + tap, length), 0:size]
            result = result + taps_ref[tap : tap + 1, columns] * shifted
        return silu(result)

    state_dim = write_ref.shape[1]
    writes = convolved(rim_w[...], write_ref[...], pl.ds(width, state_dim), state_dim)
    reads[...] = convolved(
        rim_r[...], read_ref[...], pl.ds(width + state_dim, state_dim), state_dim
    ).astype(BF16)
    for b in range(blocks):
        span = pl.ds(b * SPAN, SPAN)
        flipped = writes[b * SPAN : (b + 1) * SPAN].T.astype(BF16)
        write_t[b] = flipped
        scores[b] = jnp.where(row >= col, dot(reads[span, :], flipped), 0.0)

    def turn(i):
        return lax.rem(LANES - per_chunk * i, LANES)

    def columns_of(i):
        return pl.ds(pl.multiple_of(i * CHUNK, CHUNK), CHUNK)

    def local_state(i):
        columns = columns_of(i)
        active = convolved(rim_x[:, columns], x_ref[:, columns], columns, CHUNK).astype(BF16)
        values[:, columns] = active
        shift = turn(i)
        scaled = (active.astype(F32) * spread(tail_t[...], shift, unit[...])).astype(BF16)
        decay = spread(decays[...], shift, unit[...])
        state = dot(write_t[0], scaled[0:SPAN])
        for b in range(1, blocks):
            inner_state[b - 1, :, columns] = state
            state = decay[b : b + 1] * state + dot(write_t[b], scaled[b * SPAN : (b + 1) * SPAN])
        own_state[i] = state

    def hand_on(j):
        @pl.when(has_left)
        def _():
            passing(j).wait_recv()

        @pl.when(has_right)
        def _():
            decay = spread(decays[...], turn(j), unit[...])
            whole = decay[0:1]
            for b in range(1, blocks):
                whole = whole * decay[b : b + 1]
            leaving[j] = (whole * came[j].astype(F32) + own_state[j]).astype(BF16)
            passing(j).start()

    def inner(i):
        columns_at = i * CHUNK
        turned = pltpu.roll(cum_t[...], turn(i), 1)
        rows = pl.ds(pl.multiple_of(i * per_chunk, per_chunk), per_chunk)
        logs = cum[rows, :]
        steps = steps_ref[rows, :]
        pair = LANES // head_dim
        lane = lax.broadcasted_iota(jnp.int32, (SPAN, LANES), 1) // head_dim
        for g in range(per_chunk // pair):
            columns = pl.ds(pl.multiple_of(columns_at + g * LANES, LANES), LANES)
            for b in range(blocks):
                lo, hi = b * SPAN, (b + 1) * SPAN
                both = values[lo:hi, columns]
                mix, parts = [], []
                for q in range(pair):
                    h = g * pair + q
                    gap = turned[lo:hi, h : h + 1] - logs[h : h + 1, lo:hi]
                    m = scores[b] * jnp.exp(jnp.minimum(gap, 0.0)) * steps[h : h + 1, lo:hi]
                    mix.append(m.astype(BF16))
                    parts.append(jnp.where(lane == q, both, jnp.zeros_like(both)))
                total[lo:hi, columns] = dot(
                    jnp.concatenate(mix, axis=1), jnp.concatenate(parts, axis=0)
                )

    lag = jnp.minimum(2 * place, chunks)

    def first_half(t, _):
        local_state(t)

        @pl.when(t >= lag)
        def _():
            hand_on(t - lag)

        return 0

    def second_half(t, _):
        inner(t)

        @pl.when(t + chunks - lag < chunks)
        def _():
            hand_on(t + chunks - lag)

        return 0

    lax.fori_loop(0, chunks, first_half, 0)
    lax.fori_loop(0, chunks, second_half, 0)

    def finish(j, _):
        columns = columns_of(j)
        shift = turn(j)
        grow = spread(grow_t[...], shift, unit[...])
        decay = spread(decays[...], shift, unit[...])
        carry = came[j]
        wide = carry.astype(F32)
        skip = decay[blocks : blocks + 1]
        ahead = None
        for b in range(blocks):
            lo, hi = b * SPAN, (b + 1) * SPAN
            if b:
                ahead = decay[b - 1 : b] if ahead is None else ahead * decay[b - 1 : b]
                carry = (inner_state[b - 1, :, columns] + ahead * wide).astype(BF16)
            outer = grow[lo:hi] * dot(reads[lo:hi, :], carry)
            out = total[lo:hi, columns] + outer + skip * values[lo:hi, columns].astype(F32)
            gated = out * silu(gate_ref[lo:hi, columns].astype(F32))
            total[lo:hi, columns] = gated
            power = gated * gated
            part = power[:, 0:LANES]
            for g in range(1, CHUNK // LANES):
                part = part + power[:, g * LANES : (g + 1) * LANES]
            squares[lo:hi, :] += part
        return 0

    lax.fori_loop(0, chunks, finish, 0)
    mean = jnp.sum(squares[...], axis=1, keepdims=True) * (1.0 / width)
    scale[...] = jnp.broadcast_to(lax.rsqrt(mean + 1e-05), scale.shape)
    segments = length // SEG
    seg_row = lax.broadcasted_iota(jnp.int32, (segments, length), 0)
    seg_col = lax.broadcasted_iota(jnp.int32, (segments, length), 1) // SEG
    pool = jnp.where(seg_row == seg_col, 1.0 / SEG, 0.0).astype(BF16)

    def norm(j, _):
        columns = columns_of(j)
        normed = (total[:, columns] * scale[:, 0:1] * gain_ref[:, columns]).astype(BF16)
        mixed_ref[:, columns] = normed
        pooled_ref[:, columns] = dot(pool, normed).astype(BF16).astype(F32)
        return 0

    lax.fori_loop(0, chunks, norm, 0)

    @pl.when(has_right)
    def _():
        for copy in rims():
            copy.wait_send()

        def sent(j, _):
            passing(j).wait_send()
            return 0

        lax.fori_loop(0, chunks, sent, 0)


def code_kernel(
    n_dp,
    n_seq,
    pooled_ref,
    weight_ref,
    prior_ref,
    codes_ref,
    kernel_ref,
    blocks_in,
    part_out,
    part_in,
    all_codes,
    all_prior,
    block_send,
    block_recv,
    part_send,
    part_recv,
    code_sems,
    prior_sems,
):
    n_dev = n_dp * n_seq
    depth, code_dim = weight_ref.shape
    rows = pooled_ref.shape[0]
    group = lax.axis_index("dp")
    place = lax.axis_index("seq")
    me = group * n_seq + place

    def device(offset):
        other = lax.rem(me + offset, n_dev)
        return {"dp": other // n_seq, "seq": lax.rem(other, n_seq)}

    barrier = pltpu.get_barrier_semaphore()

    def greet(offset, _):
        pl.semaphore_signal(barrier, inc=1, device_id=device(offset), device_id_type=MESH)
        return 0

    lax.fori_loop(1, n_dev, greet, 0)
    pl.semaphore_wait(barrier, n_dev - 1)

    def block_copy(o):
        to = lax.rem(group + o, n_dp)
        return pltpu.make_async_remote_copy(
            src_ref=pooled_ref.at[:, pl.ds(pl.multiple_of(to * depth, LANES), depth)],
            dst_ref=blocks_in.at[n_dp - o],
            send_sem=block_send.at[o],
            recv_sem=block_recv.at[n_dp - o],
            device_id={"dp": to},
            device_id_type=MESH,
        )

    def part_copy(o):
        to = lax.rem(group + o, n_dp)
        return pltpu.make_async_remote_copy(
            src_ref=part_out.at[o],
            dst_ref=part_in.at[n_dp - o],
            send_sem=part_send.at[o],
            recv_sem=part_recv.at[n_dp - o],
            device_id={"dp": to},
            device_id_type=MESH,
        )

    def to_all(source, target, sems):
        def one(offset, _):
            pltpu.make_async_remote_copy(
                src_ref=source,
                dst_ref=target.at[me],
                send_sem=sems.at[0],
                recv_sem=sems.at[1],
                device_id=device(offset),
                device_id_type=MESH,
            ).start()
            return 0

        lax.fori_loop(1, n_dev, one, 0)

    def all_done(target, sems, which):
        most = target.at[pl.ds(0, n_dev - 1)]
        pltpu.make_async_copy(most, most, sems.at[which]).wait()

    for o in range(1, n_dp):
        block_copy(o).start()
    to_all(prior_ref, all_prior, prior_sems)
    all_prior[me] = prior_ref[...]
    blocks_in[0] = pooled_ref[:, pl.ds(pl.multiple_of(group * depth, LANES), depth)]
    for o in range(1, n_dp):
        block_copy(o).wait_recv()
    gathered = blocks_in[...].reshape(n_dp * rows, depth).astype(BF16)
    part_out[...] = dot(gathered, weight_ref[...]).reshape(n_dp, rows, code_dim)
    for o in range(1, n_dp):
        part_copy(o).start()
    codes = part_out[0]
    for o in range(1, n_dp):
        part_copy(o).wait_recv()
    for o in range(1, n_dp):
        codes = codes + part_in[o]
    codes_ref[...] = codes
    to_all(codes_ref, all_codes, code_sems)
    all_codes[me] = codes
    row_sq = jnp.sum(codes * codes, axis=1, keepdims=True)
    ones = jnp.ones((rows, code_dim), F32)

    def against(columns):
        flat = columns.reshape(n_dev * rows, code_dim)
        cross = lax.dot_general(codes, flat, NT, precision=HIGH, preferred_element_type=F32)
        col_sq = lax.dot_general(ones, flat * flat, NT, precision=HIGH, preferred_element_type=F32)
        return 2.0 * code_dim / (2.0 * code_dim + (row_sq + col_sq - 2.0 * cross))

    all_done(all_prior, prior_sems, 1)
    kernel_ref[:, n_dev * rows :] = against(all_prior[...])
    all_done(all_codes, code_sems, 1)
    kernel_ref[:, : n_dev * rows] = against(all_codes[...])
    all_done(all_prior, prior_sems, 0)
    all_done(all_codes, code_sems, 0)
    for o in range(1, n_dp):
        block_copy(o).wait_send()
        part_copy(o).wait_send()


def per_device(
    n_dp,
    n_seq,
    inputs,
    gate_proj,
    write_proj,
    read_proj,
    step_size,
    log_forget,
    conv_weight,
    conv_bias,
    skip_gain,
    norm_gain,
    code_weight,
    prior_draw,
):
    length, width = inputs.shape[1:]
    state_dim = write_proj.shape[2]
    heads = step_size.shape[1]
    head_dim = width // heads
    chunks = width // CHUNK
    blocks = length // SPAN
    segments = length // SEG
    code_dim = code_weight.shape[1]
    n_dev = n_dp * n_seq
    vmem = pl.BlockSpec(memory_space=pltpu.VMEM)
    mixed, pooled = pl.pallas_call(
        functools.partial(mixer_kernel, n_seq, head_dim),
        out_shape=(
            jax.ShapeDtypeStruct((length, width), BF16),
            jax.ShapeDtypeStruct((segments, width), F32),
        ),
        in_specs=[vmem] * 10,
        out_specs=(vmem, vmem),
        scratch_shapes=[
            pltpu.VMEM((16, width), BF16),
            pltpu.VMEM((16, state_dim), BF16),
            pltpu.VMEM((16, state_dim), BF16),
            pltpu.VMEM((8 + length, CHUNK), F32),
            pltpu.VMEM((length, width), BF16),
            pltpu.VMEM((length, width), F32),
            pltpu.VMEM((blocks - 1, state_dim, width), F32),
            pltpu.VMEM((chunks, state_dim, CHUNK), F32),
            pltpu.VMEM((chunks, state_dim, CHUNK), BF16),
            pltpu.VMEM((chunks, state_dim, CHUNK), BF16),
            pltpu.VMEM((LANES, length), F32),
            pltpu.VMEM((length, LANES), F32),
            pltpu.VMEM((length, LANES), F32),
            pltpu.VMEM((length, LANES), F32),
            pltpu.VMEM((16, LANES), F32),
            pltpu.VMEM((2 * LANES, CHUNK), BF16),
            pltpu.VMEM((blocks, SPAN, SPAN), F32),
            pltpu.VMEM((blocks, state_dim, SPAN), BF16),
            pltpu.VMEM((length, state_dim), BF16),
            pltpu.VMEM((length, LANES), F32),
            pltpu.VMEM((length, LANES), F32),
            pltpu.SemaphoreType.DMA((3,)),
            pltpu.SemaphoreType.DMA((3,)),
            pltpu.SemaphoreType.DMA((chunks,)),
            pltpu.SemaphoreType.DMA((chunks,)),
        ],
        compiler_params=pltpu.CompilerParams(
            collective_id=0, has_side_effects=True, vmem_limit_bytes=48 * 1024 * 1024
        ),
        name="mixer",
    )(
        inputs[0],
        gate_proj[0],
        write_proj[0],
        read_proj[0],
        step_size[0],
        log_forget[0],
        conv_weight,
        conv_bias[None, :],
        skip_gain[None, :],
        norm_gain[None, :],
    )
    codes, kernel = pl.pallas_call(
        functools.partial(code_kernel, n_dp, n_seq),
        out_shape=(
            jax.ShapeDtypeStruct((segments, code_dim), F32),
            jax.ShapeDtypeStruct((segments, 2 * n_dev * segments), F32),
        ),
        in_specs=[vmem] * 3,
        out_specs=(vmem, vmem),
        scratch_shapes=[
            pltpu.VMEM((n_dp, segments, width // n_dp), F32),
            pltpu.VMEM((n_dp, segments, code_dim), F32),
            pltpu.VMEM((n_dp, segments, code_dim), F32),
            pltpu.VMEM((n_dev, segments, code_dim), F32),
            pltpu.VMEM((n_dev, segments, code_dim), F32),
            pltpu.SemaphoreType.DMA((n_dp,)),
            pltpu.SemaphoreType.DMA((n_dp,)),
            pltpu.SemaphoreType.DMA((n_dp,)),
            pltpu.SemaphoreType.DMA((n_dp,)),
            pltpu.SemaphoreType.DMA((2,)),
            pltpu.SemaphoreType.DMA((2,)),
        ],
        compiler_params=pltpu.CompilerParams(
            collective_id=1, has_side_effects=True, vmem_limit_bytes=48 * 1024 * 1024
        ),
        name="codes",
    )(pooled, code_weight, prior_draw)
    return (mixed[None], codes, kernel)


def solution(mesh):
    in_specs = (
        P("dp", "seq", None),
        P("dp", "seq", None),
        P("dp", "seq", None),
        P("dp", "seq", None),
        P("dp", None, "seq"),
        P("dp", None, "seq"),
        P(),
        P(),
        P(),
        P(),
        P("dp", None),
        P(("dp", "seq"), None),
    )
    out_specs = (P("dp", "seq", None), P(("dp", "seq"), None), P(("dp", "seq"), None))
    return jax.shard_map(
        functools.partial(per_device, mesh.shape["dp"], mesh.shape["seq"]),
        mesh=mesh,
        in_specs=in_specs,
        out_specs=out_specs,
        check_vma=False,
    )
```

```python
import functools

import jax
import jax.numpy as jnp
from jax import lax
from jax.experimental import pallas as pl
from jax.experimental.pallas import tpu as pltpu
from jax.sharding import PartitionSpec as P

SPAN = 128
SEG = 32
LANES = 128
CHUNK = 512
F32 = jnp.float32
BF16 = jnp.bfloat16
HIGH = lax.Precision.HIGHEST
MESH = pl.DeviceIdType.MESH
NT = (((1,), (1,)), ((), ()))


def silu(v):
    half = 0.5 * v
    return half + half * jnp.tanh(half)


def dot(a, b):
    return jnp.dot(a, b, preferred_element_type=F32)


def spread(rows, shift, unit):
    turned = pltpu.roll(rows, shift, 1)
    upper = turned.astype(BF16)
    lower = (turned - upper.astype(F32)).astype(BF16)
    return dot(jnp.concatenate([upper, lower], axis=1), unit)


def mixer_kernel(
    n_seq,
    head_dim,
    x_hbm,
    gate_hbm,
    write_hbm,
    read_hbm,
    steps_hbm,
    logs_hbm,
    taps_hbm,
    bias_hbm,
    skip_hbm,
    gain_hbm,
    mixed_hbm,
    pooled_ref,
    x_ref,
    gate_ref,
    write_ref,
    read_ref,
    steps_ref,
    logs_ref,
    taps_ref,
    bias_ref,
    skip_ref,
    gain_ref,
    mixed_ref,
    rim_x,
    rim_w,
    rim_r,
    pad,
    values,
    total,
    inner_state,
    own_state,
    came,
    leaving,
    cum,
    cum_t,
    tail_t,
    grow_t,
    decays,
    unit,
    scores,
    write_t,
    reads,
    squares,
    scale,
    load_sem,
    store_sem,
    rim_send,
    rim_recv,
    send_sem,
    recv_sem,
):
    loads = [
        pltpu.make_async_copy(source, target, load_sem.at[k])
        for k, (source, target) in enumerate(
            (
                (logs_hbm, logs_ref),
                (steps_hbm, steps_ref),
                (skip_hbm, skip_ref),
                (write_hbm, write_ref),
                (read_hbm, read_ref),
                (taps_hbm, taps_ref),
                (bias_hbm, bias_ref),
                (x_hbm, x_ref),
                (gate_hbm, gate_ref),
                (gain_hbm, gain_ref),
            )
        )
    ]
    for load in loads:
        load.start()
    length, width = x_ref.shape
    heads = steps_ref.shape[0]
    taps = taps_ref.shape[0]
    chunks = width // CHUNK
    per_chunk = CHUNK // head_dim
    blocks = length // SPAN
    place = lax.axis_index("seq")
    has_left = place > 0
    has_right = place < n_seq - 1
    right = {"seq": jnp.minimum(place + 1, n_seq - 1)}
    left = {"seq": jnp.maximum(place - 1, 0)}

    barrier = pltpu.get_barrier_semaphore()

    @pl.when(has_left)
    def _():
        pl.semaphore_signal(barrier, inc=1, device_id=left, device_id_type=MESH)

    @pl.when(has_right)
    def _():
        pl.semaphore_signal(barrier, inc=1, device_id=right, device_id_type=MESH)

    neighbours = jnp.minimum(place, 1) + jnp.minimum(n_seq - 1 - place, 1)
    pl.semaphore_wait(barrier, neighbours)

    def rims():
        return [
            pltpu.make_async_remote_copy(
                src_ref=source.at[pl.ds(length - 16, 16)],
                dst_ref=target,
                send_sem=rim_send.at[k],
                recv_sem=rim_recv.at[k],
                device_id=right,
                device_id_type=MESH,
            )
            for k, (source, target) in enumerate(
                ((x_hbm, rim_x), (write_hbm, rim_w), (read_hbm, rim_r))
            )
        ]

    def passing(j):
        return pltpu.make_async_remote_copy(
            src_ref=leaving.at[j],
            dst_ref=came.at[j],
            send_sem=send_sem.at[j],
            recv_sem=recv_sem.at[j],
            device_id=right,
            device_id_type=MESH,
        )

    @pl.when(has_right)
    def _():
        for copy in rims():
            copy.start()

    for load in loads[0:3]:
        load.wait()

    row = lax.broadcasted_iota(jnp.int32, (SPAN, SPAN), 0)
    col = lax.broadcasted_iota(jnp.int32, (SPAN, SPAN), 1)
    below = (row >= col).astype(F32)
    same = (row == col).astype(F32)
    cum[...] = jnp.zeros_like(cum)
    decays[...] = jnp.zeros_like(decays)
    pad_heads = jnp.zeros((LANES - heads, SPAN), F32)
    for b in range(blocks):
        span = pl.ds(b * SPAN, SPAN)
        logs = jnp.concatenate([logs_ref[:, span], pad_heads], axis=0)
        steps = jnp.concatenate([steps_ref[:, span], pad_heads], axis=0)
        cum[:, span] = lax.dot_general(logs, below, NT, precision=HIGH, preferred_element_type=F32)
        by_time = lax.dot_general(below, logs, NT, precision=HIGH, preferred_element_type=F32)
        steps_t = lax.dot_general(same, steps, NT, precision=HIGH, preferred_element_type=F32)
        cum_t[span, :] = by_time
        grow_t[span, :] = jnp.exp(by_time)
        tail_t[span, :] = jnp.exp(jnp.minimum(by_time[SPAN - 1 :, :] - by_time, 0.0)) * steps_t
        decays[b : b + 1, :] = jnp.exp(by_time[SPAN - 1 :, :])
    decays[blocks : blocks + 1, 0:heads] = skip_ref[...]
    k = lax.broadcasted_iota(jnp.int32, (2 * LANES, CHUNK), 0)
    c = lax.broadcasted_iota(jnp.int32, (2 * LANES, CHUNK), 1)
    unit[...] = jnp.where(k % LANES == c // head_dim, 1.0, 0.0).astype(BF16)
    squares[...] = jnp.zeros_like(squares)

    for load in loads[3:8]:
        load.wait()

    @pl.when(has_left)
    def _():
        for copy in rims():
            copy.wait_recv()

    @pl.when(jnp.logical_not(has_left))
    def _():
        rim_x[...] = jnp.zeros_like(rim_x)
        rim_w[...] = jnp.zeros_like(rim_w)
        rim_r[...] = jnp.zeros_like(rim_r)
        came[...] = jnp.zeros_like(came)

    def convolved(rim, body, columns, size):
        pad[0:8, 0:size] = rim.astype(F32)[8:16]
        pad[8 : 8 + length, 0:size] = body.astype(F32)
        result = bias_ref[:, columns] + taps_ref[taps - 1 : taps, columns] * body.astype(F32)
        for tap in range(taps - 1):
            shifted = pad[pl.ds(8 - (taps - 1) + tap, length), 0:size]
            result = result + taps_ref[tap : tap + 1, columns] * shifted
        return silu(result)

    state_dim = write_ref.shape[1]
    writes = convolved(rim_w[...], write_ref[...], pl.ds(width, state_dim), state_dim)
    reads[...] = convolved(
        rim_r[...], read_ref[...], pl.ds(width + state_dim, state_dim), state_dim
    ).astype(BF16)
    for b in range(blocks):
        span = pl.ds(b * SPAN, SPAN)
        flipped = writes[b * SPAN : (b + 1) * SPAN].T.astype(BF16)
        write_t[b] = flipped
        scores[b] = jnp.where(row >= col, dot(reads[span, :], flipped), 0.0)

    def turn(i):
        return lax.rem(LANES - per_chunk * i, LANES)

    def columns_of(i):
        return pl.ds(pl.multiple_of(i * CHUNK, CHUNK), CHUNK)

    def local_state(i):
        columns = columns_of(i)
        active = convolved(rim_x[:, columns], x_ref[:, columns], columns, CHUNK).astype(BF16)
        values[:, columns] = active
        shift = turn(i)
        scaled = (active.astype(F32) * spread(tail_t[...], shift, unit[...])).astype(BF16)
        decay = spread(decays[...], shift, unit[...])
        state = dot(write_t[0], scaled[0:SPAN])
        for b in range(1, blocks):
            inner_state[b - 1, :, columns] = state
            state = decay[b : b + 1] * state + dot(write_t[b], scaled[b * SPAN : (b + 1) * SPAN])
        own_state[i] = state

    def hand_on(j):
        @pl.when(has_left)
        def _():
            passing(j).wait_recv()

        @pl.when(has_right)
        def _():
            decay = spread(decays[...], turn(j), unit[...])
            whole = decay[0:1]
            for b in range(1, blocks):
                whole = whole * decay[b : b + 1]
            leaving[j] = (whole * came[j].astype(F32) + own_state[j]).astype(BF16)
            passing(j).start()

    def inner(i):
        columns_at = i * CHUNK
        turned = pltpu.roll(cum_t[...], turn(i), 1)
        rows = pl.ds(pl.multiple_of(i * per_chunk, per_chunk), per_chunk)
        logs = cum[rows, :]
        steps = steps_ref[rows, :]
        pair = LANES // head_dim
        lane = lax.broadcasted_iota(jnp.int32, (SPAN, LANES), 1) // head_dim
        for g in range(per_chunk // pair):
            columns = pl.ds(pl.multiple_of(columns_at + g * LANES, LANES), LANES)
            for b in range(blocks):
                lo, hi = b * SPAN, (b + 1) * SPAN
                both = values[lo:hi, columns]
                mix, parts = [], []
                for q in range(pair):
                    h = g * pair + q
                    gap = turned[lo:hi, h : h + 1] - logs[h : h + 1, lo:hi]
                    m = scores[b] * jnp.exp(jnp.minimum(gap, 0.0)) * steps[h : h + 1, lo:hi]
                    mix.append(m.astype(BF16))
                    parts.append(jnp.where(lane == q, both, jnp.zeros_like(both)))
                total[lo:hi, columns] = dot(
                    jnp.concatenate(mix, axis=1), jnp.concatenate(parts, axis=0)
                )

    late = chunks + 4 * (place // 2 - 1) + lax.rem(place, 2)
    lag = jnp.minimum(jnp.where(place < 2, 2 * place, late), 2 * chunks)

    def first_half(t, _):
        local_state(t)

        @pl.when(t >= lag)
        def _():
            hand_on(t - lag)

        return 0

    def second_half(t, _):
        inner(t)

        j = t + chunks - lag

        @pl.when(jnp.logical_and(j >= 0, j < chunks))
        def _():
            hand_on(j)

        return 0

    lax.fori_loop(0, chunks, first_half, 0)
    lax.fori_loop(0, chunks, second_half, 0)

    for load in loads[8:]:
        load.wait()

    def finish(j, _):
        @pl.when(j + lag >= 2 * chunks)
        def _():
            hand_on(j)

        columns = columns_of(j)
        shift = turn(j)
        grow = spread(grow_t[...], shift, unit[...])
        decay = spread(decays[...], shift, unit[...])
        carry = came[j]
        wide = carry.astype(F32)
        skip = decay[blocks : blocks + 1]
        ahead = None
        for b in range(blocks):
            lo, hi = b * SPAN, (b + 1) * SPAN
            if b:
                ahead = decay[b - 1 : b] if ahead is None else ahead * decay[b - 1 : b]
                carry = (inner_state[b - 1, :, columns] + ahead * wide).astype(BF16)
            outer = grow[lo:hi] * dot(reads[lo:hi, :], carry)
            out = total[lo:hi, columns] + outer + skip * values[lo:hi, columns].astype(F32)
            gated = out * silu(gate_ref[lo:hi, columns].astype(F32))
            total[lo:hi, columns] = gated
            power = gated * gated
            part = power[:, 0:LANES]
            for g in range(1, CHUNK // LANES):
                part = part + power[:, g * LANES : (g + 1) * LANES]
            squares[lo:hi, :] += part
        return 0

    lax.fori_loop(0, chunks, finish, 0)
    mean = jnp.sum(squares[...], axis=1, keepdims=True) * (1.0 / width)
    scale[...] = jnp.broadcast_to(lax.rsqrt(mean + 1e-05), scale.shape)
    segments = length // SEG
    seg_row = lax.broadcasted_iota(jnp.int32, (segments, length), 0)
    seg_col = lax.broadcasted_iota(jnp.int32, (segments, length), 1) // SEG
    pool = jnp.where(seg_row == seg_col, 1.0 / SEG, 0.0).astype(BF16)

    def norm(j, _):
        columns = columns_of(j)
        normed = (total[:, columns] * scale[:, 0:1] * gain_ref[:, columns]).astype(BF16)
        mixed_ref[:, columns] = normed
        pooled_ref[:, columns] = dot(pool, normed).astype(BF16).astype(F32)
        return 0

    lax.fori_loop(0, chunks, norm, 0)
    stored = pltpu.make_async_copy(mixed_ref, mixed_hbm, store_sem)

    stored.start()

    @pl.when(has_right)
    def _():
        for copy in rims():
            copy.wait_send()

        def sent(j, _):
            passing(j).wait_send()
            return 0

        lax.fori_loop(0, chunks, sent, 0)

    stored.wait()


def code_kernel(
    n_dp,
    n_seq,
    pooled_ref,
    weight_ref,
    prior_ref,
    codes_ref,
    kernel_ref,
    blocks_in,
    part_out,
    part_in,
    gathered,
    mine,
    landed,
    prior_in,
    block_send,
    block_recv,
    part_send,
    part_recv,
    prior_send,
    prior_recv,
    code_send,
    code_recv,
):
    place = lax.axis_index("seq")
    group = lax.axis_index("dp")

    def along_dp(o):
        return {"dp": lax.rem(group + o, n_dp)}

    def along_seq(o):
        return {"seq": lax.rem(place + o, n_seq)}

    barrier = pltpu.get_barrier_semaphore()
    for o in range(1, n_seq):
        pl.semaphore_signal(barrier, inc=1, device_id=along_seq(o), device_id_type=MESH)
    for o in range(1, n_dp):
        pl.semaphore_signal(barrier, inc=1, device_id=along_dp(o), device_id_type=MESH)
    pl.semaphore_wait(barrier, n_seq + n_dp - 2)

    depth, code_dim = weight_ref.shape
    rows = pooled_ref.shape[0]

    def block_copy(o):
        start = pl.multiple_of(lax.rem(group + o, n_dp) * depth, LANES)
        return pltpu.make_async_remote_copy(
            src_ref=pooled_ref.at[:, pl.ds(start, depth)],
            dst_ref=blocks_in.at[n_dp - o],
            send_sem=block_send.at[o],
            recv_sem=block_recv.at[n_dp - o],
            device_id=along_dp(o),
            device_id_type=MESH,
        )

    def part_copy(o):
        return pltpu.make_async_remote_copy(
            src_ref=part_out,
            dst_ref=part_in.at[n_dp - o],
            send_sem=part_send.at[o],
            recv_sem=part_recv.at[n_dp - o],
            device_id=along_dp(o),
            device_id_type=MESH,
        )

    def column_copy(o):
        return pltpu.make_async_remote_copy(
            src_ref=mine,
            dst_ref=landed.at[n_seq - o],
            send_sem=code_send.at[o],
            recv_sem=code_recv.at[n_seq - o],
            device_id=along_seq(o),
            device_id_type=MESH,
        )

    for o in range(1, n_dp):
        block_copy(o).start()

    def prior_copy(o):
        return pltpu.make_async_remote_copy(
            src_ref=prior_ref,
            dst_ref=prior_in.at[n_dp - o],
            send_sem=prior_send.at[o],
            recv_sem=prior_recv.at[n_dp - o],
            device_id=along_dp(o),
            device_id_type=MESH,
        )

    for o in range(1, n_dp):
        prior_copy(o).start()
    mine[n_dp + group] = prior_ref[...]
    for o in range(1, n_dp):
        prior_copy(o).wait_recv()
    for o in range(1, n_dp):
        mine[n_dp + lax.rem(group + o, n_dp)] = prior_in[o]
    blocks_in[0] = pooled_ref[:, pl.ds(pl.multiple_of(group * depth, LANES), depth)]
    for o in range(1, n_dp):
        block_copy(o).wait_recv()
    pooled_rows = blocks_in[...].reshape(n_dp * rows, depth).astype(BF16)
    part_out[...] = dot(pooled_rows, weight_ref[...]).reshape(n_dp, rows, code_dim)
    for o in range(1, n_dp):
        part_copy(o).start()
    for o in range(1, n_dp):
        part_copy(o).wait_recv()
    summed = []
    for r in range(n_dp):
        rows_sum = part_out[r]
        for o in range(1, n_dp):
            rows_sum = rows_sum + part_in[o, (r - o) % n_dp]
        summed.append(rows_sum)
        mine[lax.rem(group + r, n_dp)] = rows_sum
    for o in range(1, n_seq):
        column_copy(o).start()
    codes = summed[0]
    codes_ref[...] = codes
    row_sq = jnp.sum(codes * codes, axis=1, keepdims=True)
    ones = jnp.ones((rows, code_dim), F32)
    for o in range(1, n_seq):
        column_copy(o).wait_recv()
    gathered[place] = mine[...]
    for o in range(1, n_seq):
        gathered[lax.rem(place + o, n_seq)] = landed[o]
    flat = jnp.concatenate(
        [gathered[q, k] for k in range(2 * n_dp) for q in range(n_seq)], axis=0
    )
    cross = lax.dot_general(codes, flat, NT, precision=HIGH, preferred_element_type=F32)
    col_sq = lax.dot_general(ones, flat * flat, NT, precision=HIGH, preferred_element_type=F32)
    kernel_ref[...] = 2.0 * code_dim / (2.0 * code_dim + (row_sq + col_sq - 2.0 * cross))

    for o in range(1, n_dp):
        prior_copy(o).wait_send()
        block_copy(o).wait_send()
        part_copy(o).wait_send()
    for o in range(1, n_seq):
        column_copy(o).wait_send()


def per_device(
    n_dp,
    n_seq,
    inputs,
    gate_proj,
    write_proj,
    read_proj,
    step_size,
    log_forget,
    conv_weight,
    conv_bias,
    skip_gain,
    norm_gain,
    code_weight,
    prior_draw,
):
    length, width = inputs.shape[1:]
    state_dim = write_proj.shape[2]
    heads = step_size.shape[1]
    head_dim = width // heads
    chunks = width // CHUNK
    blocks = length // SPAN
    segments = length // SEG
    code_dim = code_weight.shape[1]
    n_dev = n_dp * n_seq
    vmem = pl.BlockSpec(memory_space=pltpu.VMEM)
    anywhere = pl.BlockSpec(memory_space=pl.ANY)
    mixed, pooled = pl.pallas_call(
        functools.partial(mixer_kernel, n_seq, head_dim),
        out_shape=(
            jax.ShapeDtypeStruct((length, width), BF16),
            jax.ShapeDtypeStruct((segments, width), F32),
        ),
        in_specs=[anywhere] * 10,
        out_specs=(anywhere, vmem),
        scratch_shapes=[
            pltpu.VMEM((length, width), BF16),
            pltpu.VMEM((length, width), BF16),
            pltpu.VMEM((length, state_dim), BF16),
            pltpu.VMEM((length, state_dim), BF16),
            pltpu.VMEM((heads, length), F32),
            pltpu.VMEM((heads, length), F32),
            pltpu.VMEM(conv_weight.shape, F32),
            pltpu.VMEM((1, conv_bias.shape[0]), F32),
            pltpu.VMEM((1, heads), F32),
            pltpu.VMEM((1, width), F32),
            pltpu.VMEM((length, width), BF16),
            pltpu.VMEM((16, width), BF16),
            pltpu.VMEM((16, state_dim), BF16),
            pltpu.VMEM((16, state_dim), BF16),
            pltpu.VMEM((8 + length, CHUNK), F32),
            pltpu.VMEM((length, width), BF16),
            pltpu.VMEM((length, width), F32),
            pltpu.VMEM((blocks - 1, state_dim, width), F32),
            pltpu.VMEM((chunks, state_dim, CHUNK), F32),
            pltpu.VMEM((chunks, state_dim, CHUNK), BF16),
            pltpu.VMEM((chunks, state_dim, CHUNK), BF16),
            pltpu.VMEM((LANES, length), F32),
            pltpu.VMEM((length, LANES), F32),
            pltpu.VMEM((length, LANES), F32),
            pltpu.VMEM((length, LANES), F32),
            pltpu.VMEM((16, LANES), F32),
            pltpu.VMEM((2 * LANES, CHUNK), BF16),
            pltpu.VMEM((blocks, SPAN, SPAN), F32),
            pltpu.VMEM((blocks, state_dim, SPAN), BF16),
            pltpu.VMEM((length, state_dim), BF16),
            pltpu.VMEM((length, LANES), F32),
            pltpu.VMEM((length, LANES), F32),
            pltpu.SemaphoreType.DMA((11,)),
            pltpu.SemaphoreType.DMA,
            pltpu.SemaphoreType.DMA((3,)),
            pltpu.SemaphoreType.DMA((3,)),
            pltpu.SemaphoreType.DMA((chunks,)),
            pltpu.SemaphoreType.DMA((chunks,)),
        ],
        compiler_params=pltpu.CompilerParams(
            collective_id=0, has_side_effects=True, vmem_limit_bytes=60 * 1024 * 1024
        ),
        name="mixer",
    )(
        inputs[0],
        gate_proj[0],
        write_proj[0],
        read_proj[0],
        step_size[0],
        log_forget[0],
        conv_weight,
        conv_bias[None, :],
        skip_gain[None, :],
        norm_gain[None, :],
    )
    codes, kernel = pl.pallas_call(
        functools.partial(code_kernel, n_dp, n_seq),
        out_shape=(
            jax.ShapeDtypeStruct((segments, code_dim), F32),
            jax.ShapeDtypeStruct((segments, 2 * n_dev * segments), F32),
        ),
        in_specs=[vmem] * 3,
        out_specs=(vmem, vmem),
        scratch_shapes=[
            pltpu.VMEM((n_dp, segments, width // n_dp), F32),
            pltpu.VMEM((n_dp, segments, code_dim), F32),
            pltpu.VMEM((n_dp, n_dp, segments, code_dim), F32),
            pltpu.VMEM((n_seq, 2 * n_dp, segments, code_dim), F32),
            pltpu.VMEM((2 * n_dp, segments, code_dim), F32),
            pltpu.VMEM((n_seq, 2 * n_dp, segments, code_dim), F32),
            pltpu.VMEM((n_dp, segments, code_dim), F32),
            pltpu.SemaphoreType.DMA((n_dp,)),
            pltpu.SemaphoreType.DMA((n_dp,)),
            pltpu.SemaphoreType.DMA((n_dp,)),
            pltpu.SemaphoreType.DMA((n_dp,)),
            pltpu.SemaphoreType.DMA((n_dp,)),
            pltpu.SemaphoreType.DMA((n_dp,)),
            pltpu.SemaphoreType.DMA((n_seq,)),
            pltpu.SemaphoreType.DMA((n_seq,)),
        ],
        compiler_params=pltpu.CompilerParams(
            collective_id=1, has_side_effects=True, vmem_limit_bytes=48 * 1024 * 1024
        ),
        name="codes",
    )(pooled, code_weight, prior_draw)
    return (mixed[None], codes, kernel)


def solution(mesh):
    in_specs = (
        P("dp", "seq", None),
        P("dp", "seq", None),
        P("dp", "seq", None),
        P("dp", "seq", None),
        P("dp", None, "seq"),
        P("dp", None, "seq"),
        P(),
        P(),
        P(),
        P(),
        P("dp", None),
        P(("dp", "seq"), None),
    )
    out_specs = (P("dp", "seq", None), P(("dp", "seq"), None), P(("dp", "seq"), None))
    return jax.shard_map(
        functools.partial(per_device, mesh.shape["dp"], mesh.shape["seq"]),
        mesh=mesh,
        in_specs=in_specs,
        out_specs=out_specs,
        check_vma=False,
    )
```

```python
import functools

import jax
import jax.numpy as jnp
from jax import lax
from jax.experimental import pallas as pl
from jax.experimental.pallas import tpu as pltpu
from jax.sharding import PartitionSpec as P

SPAN = 128
SEG = 32
LANES = 128
CHUNK = 512
F32 = jnp.float32
BF16 = jnp.bfloat16
HIGH = lax.Precision.HIGHEST
MESH = pl.DeviceIdType.MESH
NT = (((1,), (1,)), ((), ()))


def silu(v):
    half = 0.5 * v
    return half + half * jnp.tanh(half)


def dot(a, b):
    return jnp.dot(a, b, preferred_element_type=F32)


def spread(rows, shift, unit):
    turned = pltpu.roll(rows, shift, 1)
    upper = turned.astype(BF16)
    lower = (turned - upper.astype(F32)).astype(BF16)
    return dot(jnp.concatenate([upper, lower], axis=1), unit)


def mixer_kernel(
    n_seq,
    head_dim,
    x_hbm,
    gate_hbm,
    write_hbm,
    read_hbm,
    steps_hbm,
    logs_hbm,
    taps_hbm,
    bias_hbm,
    skip_hbm,
    gain_hbm,
    mixed_hbm,
    pooled_ref,
    x_ref,
    gate_ref,
    write_ref,
    read_ref,
    steps_ref,
    logs_ref,
    taps_ref,
    bias_ref,
    skip_ref,
    gain_ref,
    mixed_ref,
    rim_x,
    rim_w,
    rim_r,
    pad,
    values,
    total,
    inner_state,
    own_state,
    came,
    leaving,
    cum,
    cum_t,
    tail_t,
    grow_t,
    decays,
    unit,
    scores,
    write_t,
    reads,
    squares,
    scale,
    load_sem,
    store_sem,
    rim_send,
    rim_recv,
    send_sem,
    recv_sem,
):
    loads = [
        pltpu.make_async_copy(source, target, load_sem.at[k])
        for k, (source, target) in enumerate(
            (
                (logs_hbm, logs_ref),
                (steps_hbm, steps_ref),
                (skip_hbm, skip_ref),
                (write_hbm, write_ref),
                (read_hbm, read_ref),
                (taps_hbm, taps_ref),
                (bias_hbm, bias_ref),
                (x_hbm, x_ref),
                (gate_hbm, gate_ref),
                (gain_hbm, gain_ref),
            )
        )
    ]
    for load in loads:
        load.start()
    length, width = x_ref.shape
    heads = steps_ref.shape[0]
    taps = taps_ref.shape[0]
    chunks = width // CHUNK
    per_chunk = CHUNK // head_dim
    blocks = length // SPAN
    place = lax.axis_index("seq")
    has_left = place > 0
    has_right = place < n_seq - 1
    right = {"seq": jnp.minimum(place + 1, n_seq - 1)}
    left = {"seq": jnp.maximum(place - 1, 0)}

    barrier = pltpu.get_barrier_semaphore()

    @pl.when(has_left)
    def _():
        pl.semaphore_signal(barrier, inc=1, device_id=left, device_id_type=MESH)

    @pl.when(has_right)
    def _():
        pl.semaphore_signal(barrier, inc=1, device_id=right, device_id_type=MESH)

    neighbours = jnp.minimum(place, 1) + jnp.minimum(n_seq - 1 - place, 1)
    pl.semaphore_wait(barrier, neighbours)

    def rims():
        return [
            pltpu.make_async_remote_copy(
                src_ref=source.at[pl.ds(length - 16, 16)],
                dst_ref=target,
                send_sem=rim_send.at[k],
                recv_sem=rim_recv.at[k],
                device_id=right,
                device_id_type=MESH,
            )
            for k, (source, target) in enumerate(
                ((x_hbm, rim_x), (write_hbm, rim_w), (read_hbm, rim_r))
            )
        ]

    def passing(j):
        return pltpu.make_async_remote_copy(
            src_ref=leaving.at[j],
            dst_ref=came.at[j],
            send_sem=send_sem.at[j],
            recv_sem=recv_sem.at[j],
            device_id=right,
            device_id_type=MESH,
        )

    @pl.when(has_right)
    def _():
        for copy in rims():
            copy.start()

    for load in loads[0:3]:
        load.wait()

    row = lax.broadcasted_iota(jnp.int32, (SPAN, SPAN), 0)
    col = lax.broadcasted_iota(jnp.int32, (SPAN, SPAN), 1)
    below = (row >= col).astype(F32)
    same = (row == col).astype(F32)
    cum[...] = jnp.zeros_like(cum)
    decays[...] = jnp.zeros_like(decays)
    pad_heads = jnp.zeros((LANES - heads, SPAN), F32)
    for b in range(blocks):
        span = pl.ds(b * SPAN, SPAN)
        logs = jnp.concatenate([logs_ref[:, span], pad_heads], axis=0)
        steps = jnp.concatenate([steps_ref[:, span], pad_heads], axis=0)
        cum[:, span] = lax.dot_general(logs, below, NT, precision=HIGH, preferred_element_type=F32)
        by_time = lax.dot_general(below, logs, NT, precision=HIGH, preferred_element_type=F32)
        steps_t = lax.dot_general(same, steps, NT, precision=HIGH, preferred_element_type=F32)
        cum_t[span, :] = by_time
        grow_t[span, :] = jnp.exp(by_time)
        tail_t[span, :] = jnp.exp(jnp.minimum(by_time[SPAN - 1 :, :] - by_time, 0.0)) * steps_t
        decays[b : b + 1, :] = jnp.exp(by_time[SPAN - 1 :, :])
    decays[blocks : blocks + 1, 0:heads] = skip_ref[...]
    k = lax.broadcasted_iota(jnp.int32, (2 * LANES, CHUNK), 0)
    c = lax.broadcasted_iota(jnp.int32, (2 * LANES, CHUNK), 1)
    unit[...] = jnp.where(k % LANES == c // head_dim, 1.0, 0.0).astype(BF16)
    squares[...] = jnp.zeros_like(squares)

    for load in loads[3:8]:
        load.wait()

    @pl.when(has_left)
    def _():
        for copy in rims():
            copy.wait_recv()

    @pl.when(jnp.logical_not(has_left))
    def _():
        rim_x[...] = jnp.zeros_like(rim_x)
        rim_w[...] = jnp.zeros_like(rim_w)
        rim_r[...] = jnp.zeros_like(rim_r)
        came[...] = jnp.zeros_like(came)

    def convolved(rim, body, columns, size):
        pad[0:8, 0:size] = rim.astype(F32)[8:16]
        pad[8 : 8 + length, 0:size] = body.astype(F32)
        result = bias_ref[:, columns] + taps_ref[taps - 1 : taps, columns] * body.astype(F32)
        for tap in range(taps - 1):
            shifted = pad[pl.ds(8 - (taps - 1) + tap, length), 0:size]
            result = result + taps_ref[tap : tap + 1, columns] * shifted
        return silu(result)

    state_dim = write_ref.shape[1]
    writes = convolved(rim_w[...], write_ref[...], pl.ds(width, state_dim), state_dim)
    reads[...] = convolved(
        rim_r[...], read_ref[...], pl.ds(width + state_dim, state_dim), state_dim
    ).astype(BF16)
    for b in range(blocks):
        span = pl.ds(b * SPAN, SPAN)
        flipped = writes[b * SPAN : (b + 1) * SPAN].T.astype(BF16)
        write_t[b] = flipped
        scores[b] = jnp.where(row >= col, dot(reads[span, :], flipped), 0.0)

    def turn(i):
        return lax.rem(LANES - per_chunk * i, LANES)

    def columns_of(i):
        return pl.ds(pl.multiple_of(i * CHUNK, CHUNK), CHUNK)

    def local_state(i):
        columns = columns_of(i)
        active = convolved(rim_x[:, columns], x_ref[:, columns], columns, CHUNK).astype(BF16)
        values[:, columns] = active
        shift = turn(i)
        scaled = (active.astype(F32) * spread(tail_t[...], shift, unit[...])).astype(BF16)
        decay = spread(decays[...], shift, unit[...])
        state = dot(write_t[0], scaled[0:SPAN])
        for b in range(1, blocks):
            inner_state[b - 1, :, columns] = state
            state = decay[b : b + 1] * state + dot(write_t[b], scaled[b * SPAN : (b + 1) * SPAN])
        own_state[i] = state

    def hand_on(j):
        @pl.when(has_left)
        def _():
            passing(j).wait_recv()

        @pl.when(has_right)
        def _():
            decay = spread(decays[...], turn(j), unit[...])
            whole = decay[0:1]
            for b in range(1, blocks):
                whole = whole * decay[b : b + 1]
            leaving[j] = (whole * came[j].astype(F32) + own_state[j]).astype(BF16)
            passing(j).start()

    def inner(i):
        columns_at = i * CHUNK
        turned = pltpu.roll(cum_t[...], turn(i), 1)
        rows = pl.ds(pl.multiple_of(i * per_chunk, per_chunk), per_chunk)
        logs = cum[rows, :]
        steps = steps_ref[rows, :]
        pair = LANES // head_dim
        lane = lax.broadcasted_iota(jnp.int32, (SPAN, LANES), 1) // head_dim
        for g in range(per_chunk // pair):
            columns = pl.ds(pl.multiple_of(columns_at + g * LANES, LANES), LANES)
            for b in range(blocks):
                lo, hi = b * SPAN, (b + 1) * SPAN
                both = values[lo:hi, columns]
                mix, parts = [], []
                for q in range(pair):
                    h = g * pair + q
                    gap = turned[lo:hi, h : h + 1] - logs[h : h + 1, lo:hi]
                    m = scores[b] * jnp.exp(jnp.minimum(gap, 0.0)) * steps[h : h + 1, lo:hi]
                    mix.append(m.astype(BF16))
                    parts.append(jnp.where(lane == q, both, jnp.zeros_like(both)))
                total[lo:hi, columns] = dot(
                    jnp.concatenate(mix, axis=1), jnp.concatenate(parts, axis=0)
                )

    lag = jnp.minimum(2 * place, chunks)

    def first_half(t, _):
        local_state(t)

        @pl.when(t >= lag)
        def _():
            hand_on(t - lag)

        return 0

    def second_half(t, _):
        inner(t)

        j = t + chunks - lag

        @pl.when(jnp.logical_and(j >= 0, j < chunks))
        def _():
            hand_on(j)

        return 0

    lax.fori_loop(0, chunks, first_half, 0)
    lax.fori_loop(0, chunks, second_half, 0)

    for load in loads[8:]:
        load.wait()

    def finish(j, _):
        @pl.when(j + lag >= 2 * chunks)
        def _():
            hand_on(j)

        columns = columns_of(j)
        shift = turn(j)
        grow = spread(grow_t[...], shift, unit[...])
        decay = spread(decays[...], shift, unit[...])
        carry = came[j]
        wide = carry.astype(F32)
        skip = decay[blocks : blocks + 1]
        ahead = None
        for b in range(blocks):
            lo, hi = b * SPAN, (b + 1) * SPAN
            if b:
                ahead = decay[b - 1 : b] if ahead is None else ahead * decay[b - 1 : b]
                carry = (inner_state[b - 1, :, columns] + ahead * wide).astype(BF16)
            outer = grow[lo:hi] * dot(reads[lo:hi, :], carry)
            out = total[lo:hi, columns] + outer + skip * values[lo:hi, columns].astype(F32)
            gated = out * silu(gate_ref[lo:hi, columns].astype(F32))
            total[lo:hi, columns] = gated
            power = gated * gated
            part = power[:, 0:LANES]
            for g in range(1, CHUNK // LANES):
                part = part + power[:, g * LANES : (g + 1) * LANES]
            squares[lo:hi, :] += part
        return 0

    lax.fori_loop(0, chunks, finish, 0)
    mean = jnp.sum(squares[...], axis=1, keepdims=True) * (1.0 / width)
    scale[...] = jnp.broadcast_to(lax.rsqrt(mean + 1e-05), scale.shape)
    segments = length // SEG
    seg_row = lax.broadcasted_iota(jnp.int32, (segments, length), 0)
    seg_col = lax.broadcasted_iota(jnp.int32, (segments, length), 1) // SEG
    pool = jnp.where(seg_row == seg_col, 1.0 / SEG, 0.0).astype(BF16)

    def norm(j, _):
        columns = columns_of(j)
        normed = (total[:, columns] * scale[:, 0:1] * gain_ref[:, columns]).astype(BF16)
        mixed_ref[:, columns] = normed
        pooled_ref[:, columns] = dot(pool, normed).astype(BF16).astype(F32)
        return 0

    lax.fori_loop(0, chunks, norm, 0)
    stored = pltpu.make_async_copy(mixed_ref, mixed_hbm, store_sem)

    stored.start()

    @pl.when(has_right)
    def _():
        for copy in rims():
            copy.wait_send()

        def sent(j, _):
            passing(j).wait_send()
            return 0

        lax.fori_loop(0, chunks, sent, 0)

    stored.wait()


def code_kernel(
    n_dp,
    n_seq,
    pooled_ref,
    weight_ref,
    prior_ref,
    codes_ref,
    kernel_ref,
    blocks_in,
    part_out,
    part_in,
    gathered,
    mine,
    landed,
    prior_in,
    block_send,
    block_recv,
    part_send,
    part_recv,
    prior_send,
    prior_recv,
    code_send,
    code_recv,
):
    place = lax.axis_index("seq")
    group = lax.axis_index("dp")

    def along_dp(o):
        return {"dp": lax.rem(group + o, n_dp)}

    def along_seq(o):
        return {"seq": lax.rem(place + o, n_seq)}

    barrier = pltpu.get_barrier_semaphore()
    for o in range(1, n_seq):
        pl.semaphore_signal(barrier, inc=1, device_id=along_seq(o), device_id_type=MESH)
    for o in range(1, n_dp):
        pl.semaphore_signal(barrier, inc=1, device_id=along_dp(o), device_id_type=MESH)
    pl.semaphore_wait(barrier, n_seq + n_dp - 2)

    depth, code_dim = weight_ref.shape
    rows = pooled_ref.shape[0]

    def block_copy(o):
        start = pl.multiple_of(lax.rem(group + o, n_dp) * depth, LANES)
        return pltpu.make_async_remote_copy(
            src_ref=pooled_ref.at[:, pl.ds(start, depth)],
            dst_ref=blocks_in.at[n_dp - o],
            send_sem=block_send.at[o],
            recv_sem=block_recv.at[n_dp - o],
            device_id=along_dp(o),
            device_id_type=MESH,
        )

    def part_copy(o):
        return pltpu.make_async_remote_copy(
            src_ref=part_out,
            dst_ref=part_in.at[n_dp - o],
            send_sem=part_send.at[o],
            recv_sem=part_recv.at[n_dp - o],
            device_id=along_dp(o),
            device_id_type=MESH,
        )

    def column_copy(o):
        return pltpu.make_async_remote_copy(
            src_ref=mine,
            dst_ref=landed.at[n_seq - o],
            send_sem=code_send.at[o],
            recv_sem=code_recv.at[n_seq - o],
            device_id=along_seq(o),
            device_id_type=MESH,
        )

    for o in range(1, n_dp):
        block_copy(o).start()

    def prior_copy(o):
        return pltpu.make_async_remote_copy(
            src_ref=prior_ref,
            dst_ref=prior_in.at[n_dp - o],
            send_sem=prior_send.at[o],
            recv_sem=prior_recv.at[n_dp - o],
            device_id=along_dp(o),
            device_id_type=MESH,
        )

    for o in range(1, n_dp):
        prior_copy(o).start()
    mine[n_dp + group] = prior_ref[...]
    for o in range(1, n_dp):
        prior_copy(o).wait_recv()
    for o in range(1, n_dp):
        mine[n_dp + lax.rem(group + o, n_dp)] = prior_in[o]
    blocks_in[0] = pooled_ref[:, pl.ds(pl.multiple_of(group * depth, LANES), depth)]
    for o in range(1, n_dp):
        block_copy(o).wait_recv()
    pooled_rows = blocks_in[...].reshape(n_dp * rows, depth).astype(BF16)
    part_out[...] = dot(pooled_rows, weight_ref[...]).reshape(n_dp, rows, code_dim)
    for o in range(1, n_dp):
        part_copy(o).start()
    for o in range(1, n_dp):
        part_copy(o).wait_recv()
    summed = []
    for r in range(n_dp):
        rows_sum = part_out[r]
        for o in range(1, n_dp):
            rows_sum = rows_sum + part_in[o, (r - o) % n_dp]
        summed.append(rows_sum)
        mine[lax.rem(group + r, n_dp)] = rows_sum
    for o in range(1, n_seq):
        column_copy(o).start()
    codes = summed[0]
    codes_ref[...] = codes
    row_sq = jnp.sum(codes * codes, axis=1, keepdims=True)
    ones = jnp.ones((rows, code_dim), F32)
    for o in range(1, n_seq):
        column_copy(o).wait_recv()
    gathered[place] = mine[...]
    for o in range(1, n_seq):
        gathered[lax.rem(place + o, n_seq)] = landed[o]
    flat = jnp.concatenate(
        [gathered[q, k] for k in range(2 * n_dp) for q in range(n_seq)], axis=0
    )
    cross = lax.dot_general(codes, flat, NT, precision=HIGH, preferred_element_type=F32)
    col_sq = lax.dot_general(ones, flat * flat, NT, precision=HIGH, preferred_element_type=F32)
    kernel_ref[...] = 2.0 * code_dim / (2.0 * code_dim + (row_sq + col_sq - 2.0 * cross))

    for o in range(1, n_dp):
        prior_copy(o).wait_send()
        block_copy(o).wait_send()
        part_copy(o).wait_send()
    for o in range(1, n_seq):
        column_copy(o).wait_send()


def per_device(
    n_dp,
    n_seq,
    inputs,
    gate_proj,
    write_proj,
    read_proj,
    step_size,
    log_forget,
    conv_weight,
    conv_bias,
    skip_gain,
    norm_gain,
    code_weight,
    prior_draw,
):
    length, width = inputs.shape[1:]
    state_dim = write_proj.shape[2]
    heads = step_size.shape[1]
    head_dim = width // heads
    chunks = width // CHUNK
    blocks = length // SPAN
    segments = length // SEG
    code_dim = code_weight.shape[1]
    n_dev = n_dp * n_seq
    vmem = pl.BlockSpec(memory_space=pltpu.VMEM)
    anywhere = pl.BlockSpec(memory_space=pl.ANY)
    mixed, pooled = pl.pallas_call(
        functools.partial(mixer_kernel, n_seq, head_dim),
        out_shape=(
            jax.ShapeDtypeStruct((length, width), BF16),
            jax.ShapeDtypeStruct((segments, width), F32),
        ),
        in_specs=[anywhere] * 10,
        out_specs=(anywhere, vmem),
        scratch_shapes=[
            pltpu.VMEM((length, width), BF16),
            pltpu.VMEM((length, width), BF16),
            pltpu.VMEM((length, state_dim), BF16),
            pltpu.VMEM((length, state_dim), BF16),
            pltpu.VMEM((heads, length), F32),
            pltpu.VMEM((heads, length), F32),
            pltpu.VMEM(conv_weight.shape, F32),
            pltpu.VMEM((1, conv_bias.shape[0]), F32),
            pltpu.VMEM((1, heads), F32),
            pltpu.VMEM((1, width), F32),
            pltpu.VMEM((length, width), BF16),
            pltpu.VMEM((16, width), BF16),
            pltpu.VMEM((16, state_dim), BF16),
            pltpu.VMEM((16, state_dim), BF16),
            pltpu.VMEM((8 + length, CHUNK), F32),
            pltpu.VMEM((length, width), BF16),
            pltpu.VMEM((length, width), F32),
            pltpu.VMEM((blocks - 1, state_dim, width), F32),
            pltpu.VMEM((chunks, state_dim, CHUNK), F32),
            pltpu.VMEM((chunks, state_dim, CHUNK), BF16),
            pltpu.VMEM((chunks, state_dim, CHUNK), BF16),
            pltpu.VMEM((LANES, length), F32),
            pltpu.VMEM((length, LANES), F32),
            pltpu.VMEM((length, LANES), F32),
            pltpu.VMEM((length, LANES), F32),
            pltpu.VMEM((16, LANES), F32),
            pltpu.VMEM((2 * LANES, CHUNK), BF16),
            pltpu.VMEM((blocks, SPAN, SPAN), F32),
            pltpu.VMEM((blocks, state_dim, SPAN), BF16),
            pltpu.VMEM((length, state_dim), BF16),
            pltpu.VMEM((length, LANES), F32),
            pltpu.VMEM((length, LANES), F32),
            pltpu.SemaphoreType.DMA((11,)),
            pltpu.SemaphoreType.DMA,
            pltpu.SemaphoreType.DMA((3,)),
            pltpu.SemaphoreType.DMA((3,)),
            pltpu.SemaphoreType.DMA((chunks,)),
            pltpu.SemaphoreType.DMA((chunks,)),
        ],
        compiler_params=pltpu.CompilerParams(
            collective_id=0, has_side_effects=True, vmem_limit_bytes=60 * 1024 * 1024
        ),
        name="mixer",
    )(
        inputs[0],
        gate_proj[0],
        write_proj[0],
        read_proj[0],
        step_size[0],
        log_forget[0],
        conv_weight,
        conv_bias[None, :],
        skip_gain[None, :],
        norm_gain[None, :],
    )
    codes, kernel = pl.pallas_call(
        functools.partial(code_kernel, n_dp, n_seq),
        out_shape=(
            jax.ShapeDtypeStruct((segments, code_dim), F32),
            jax.ShapeDtypeStruct((segments, 2 * n_dev * segments), F32),
        ),
        in_specs=[vmem] * 3,
        out_specs=(vmem, vmem),
        scratch_shapes=[
            pltpu.VMEM((n_dp, segments, width // n_dp), F32),
            pltpu.VMEM((n_dp, segments, code_dim), F32),
            pltpu.VMEM((n_dp, n_dp, segments, code_dim), F32),
            pltpu.VMEM((n_seq, 2 * n_dp, segments, code_dim), F32),
            pltpu.VMEM((2 * n_dp, segments, code_dim), F32),
            pltpu.VMEM((n_seq, 2 * n_dp, segments, code_dim), F32),
            pltpu.VMEM((n_dp, segments, code_dim), F32),
            pltpu.SemaphoreType.DMA((n_dp,)),
            pltpu.SemaphoreType.DMA((n_dp,)),
            pltpu.SemaphoreType.DMA((n_dp,)),
            pltpu.SemaphoreType.DMA((n_dp,)),
            pltpu.SemaphoreType.DMA((n_dp,)),
            pltpu.SemaphoreType.DMA((n_dp,)),
            pltpu.SemaphoreType.DMA((n_seq,)),
            pltpu.SemaphoreType.DMA((n_seq,)),
        ],
        compiler_params=pltpu.CompilerParams(
            collective_id=1, has_side_effects=True, vmem_limit_bytes=48 * 1024 * 1024
        ),
        name="codes",
    )(pooled, code_weight, prior_draw)
    return (mixed[None], codes, kernel)


def solution(mesh):
    in_specs = (
        P("dp", "seq", None),
        P("dp", "seq", None),
        P("dp", "seq", None),
        P("dp", "seq", None),
        P("dp", None, "seq"),
        P("dp", None, "seq"),
        P(),
        P(),
        P(),
        P(),
        P("dp", None),
        P(("dp", "seq"), None),
    )
    out_specs = (P("dp", "seq", None), P(("dp", "seq"), None), P(("dp", "seq"), None))
    return jax.shard_map(
        functools.partial(per_device, mesh.shape["dp"], mesh.shape["seq"]),
        mesh=mesh,
        in_specs=in_specs,
        out_specs=out_specs,
        check_vma=False,
    )
```
